32 devices in a mesh: grp: 2 (over x), dp: 16 (over z, y, core).
Axes of the slice: x: 2, y: 2, z: 4, core: 2. Of those that a mesh axis runs over, the one named last changes fastest.
Arguments:
- inputs: bfloat16 [8192, 8192], P('grp', 'dp'), parts along dimension 0, may hold values from -6 to 6
- out_grads: bfloat16 [8192, 28672], P('grp', 'dp'), parts along dimension 0, may hold values from -6 to 6
- in_basis: bfloat16 [8192, 64], P('dp'), may hold values from -0.0625 to 0.0625
- out_basis: bfloat16 [28672, 64], P('dp'), may hold values from -0.03125 to 0.03125
- example_ids: int32 [32, 256], P(('grp', 'dp')), parts along dimension 0, may hold values from 0 to 15, never falling along the last dimension, each value on 1 to 32 neighbouring positions
- loss_counts: int32 [32, 16], P(('grp', 'dp')), parts along dimension 0, may hold values from 1 to 32
- queries: bfloat16 [2048, 4096], P('dp'), may hold values from -0.09375 to 0.09375
Outputs:
- scores: float32 [512, 2048], P(('grp', 'dp')), parts along dimension 0
The draws below stay inside these ranges and needn't reach their ends.
There are 2 independent parts, one for each index of `grp`. The reference program is written for one: setup_inputs(seed, part) draws one part's arguments, and reference() takes and returns one part's arrays. A program takes and returns all parts, laid end to end along the dimension named above; an argument that names none is the same for every part. Nothing has to cross between parts.
Inputs may be any that keep to these rules, and one draw needn't show every extreme that they name: `example_ids`: each row lists the examples of one device's tokens, never falling, every example 1 to 32 tokens, one exactly 32.
All inputs are finite; a program needn't handle non-finite values.
Results may differ from the reference program's by a relative error of at most 0.0049.
Values may be sent and summed in bfloat16 or wider, within the bound.
A program may use at most 128 MiB of HBM per device.

```python
import math
import jax
import jax.numpy as jnp
import numpy as np
from jax import lax

D = 8192
FF = 28672
R = 64
TOK_DEV = 256
EX_DEV = 16
MOST = 32
TOKENS = 4096
NQ = 2048


def with_ends(result, rng, least, high):
    spot = [jax.random.randint(jax.random.fold_in(rng, axis), (), 0, length) for axis, length in enumerate(result.shape)]
    widest = result.shape.index(max(result.shape))
    next_to = spot[:widest] + [(spot[widest] + 1) % result.shape[widest]] + spot[widest + 1:]
    return result.at[tuple(spot)].set(least).at[tuple(next_to)].set(high)


def with_spikes(entries, stream_key, source, target, parts, factor):
    owner, partner = [(jnp.arange(entries.shape[axis_at]) // (entries.shape[axis_at] // parts)).reshape([-1 if axis == axis_at else 1 for axis in range(entries.ndim)]) for axis_at in (source, target)]
    chosen = jax.random.permutation(stream_key, parts)[partner]
    strong = (owner == chosen) | (owner == (partner + parts // 2) % parts)
    return jnp.where(strong, factor * entries, entries)


def block_levels(key, shape, cuts, least, largest):
    loudness, own = 1.0, jax.random.fold_in(key, 6)
    for axis_at, blocks in cuts:
        heights = jnp.exp(jax.random.uniform(jax.random.fold_in(own, axis_at), (blocks,), jnp.float32, least / len(cuts), largest / len(cuts)))
        loudness = loudness * jnp.repeat(heights, shape[axis_at] // blocks).reshape([-1 if axis == axis_at else 1 for axis in range(len(shape))])
    return loudness


def split_up(amount, total, bound, slope):
    loads = [(1 << 20) // math.isqrt(grade ** slope) + 1 for grade in range(2, amount + 1)]
    spare, holding = total - bound - (amount - 1), [1] * (amount - 1)
    while spare > 0:
        movable = [i for i in range(amount - 1) if holding[i] < bound]
        mass, left = sum([loads[i] for i in movable]), spare
        for i in movable:
            addition = min(bound - holding[i], max(1, left * loads[i] // mass), spare)
            holding[i] = holding[i] + addition
            spare = spare - addition
    return np.array([bound] + holding)


def ragged_sizes(rng, amount, total, most, skew):
    if amount == 2:
        one = jax.random.randint(rng, (), max(1, total - most), min(most, total - 1) + 1)
        return jnp.stack([one, total - one])
    sizes = jnp.asarray(split_up(amount, total, most, skew), jnp.int32)
    twos = (amount - 1) // 2
    source_of, sink = sizes[1:1 + 2 * twos:2], sizes[2:2 + 2 * twos:2]
    room = jnp.minimum(source_of - 1, most - sink)
    shifted = jax.random.randint(jax.random.fold_in(rng, 1), (twos,), 0, 1 << 20) % (room + 1)
    sizes = sizes.at[1:1 + 2 * twos:2].set(source_of - shifted).at[2:2 + 2 * twos:2].set(sink + shifted)
    return sizes[jax.random.permutation(jax.random.fold_in(rng, 2), amount)]


def normal_values(key, extent, deviation, limit, pieces=(), kind=jnp.bfloat16):
    entries = deviation * jax.random.normal(key, extent, jnp.float32)
    if pieces:
        entries = entries * block_levels(key, extent, pieces, -0.22, 0.18)
    return jnp.clip(entries, -limit, limit).astype(kind)


def bell_draw_with(own_key, dims, spread, limit, split, heavy, kind=jnp.bfloat16):
    entries = spread * jax.random.normal(own_key, dims, jnp.float32)
    if split:
        entries = entries * block_levels(own_key, dims, split, -0.22, 0.18)
    return jnp.clip(with_spikes(entries, jax.random.fold_in(own_key, 3), *heavy), -limit, limit).astype(kind)


def setup_inputs(seed: int = 0, part: int = 0) -> dict:
    keys = jax.random.split(jax.random.key(seed), 8)
    own_keys = jax.random.split(jax.random.fold_in(keys[7], part), 8)
    inputs = bell_draw_with(own_keys[0], (TOKENS, D), 1.0, 6.0, ((1, 16),), (1, 0, 16, 2.0))
    out_grads = bell_draw_with(own_keys[1], (TOKENS, FF), 1.0, 6.0, ((1, 16),), (1, 0, 16, 2.0))
    in_basis = normal_values(keys[2], (D, R), D ** -0.5, 0.0625, ((0, 16),))
    out_basis = normal_values(keys[3], (FF, R), FF ** -0.5, 0.03125, ((0, 16),))
    example_ids = jax.vmap(lambda own: jnp.searchsorted(jnp.cumsum(ragged_sizes(own, EX_DEV, TOK_DEV, MOST, 0)), jnp.arange(TOK_DEV), side="right"))(jax.random.split(own_keys[4], (TOKENS // TOK_DEV))).reshape((TOKENS // TOK_DEV, TOK_DEV)).astype(jnp.int32)
    loss_counts = with_ends(jax.random.randint(own_keys[5], (TOKENS // TOK_DEV, EX_DEV), 1, MOST + 1), jax.random.fold_in(own_keys[5], 1), 1, MOST).astype(jnp.int32)
    queries = normal_values(keys[6], (NQ, R * R), (R * R) ** -0.5, 0.09375, ((0, 16),))
    return dict(inputs=inputs, out_grads=out_grads, in_basis=in_basis, out_basis=out_basis, example_ids=example_ids, loss_counts=loss_counts, queries=queries)


def reference(inputs, out_grads, in_basis, out_basis, example_ids, loss_counts, queries):
    in_proj = jnp.dot(inputs, in_basis, preferred_element_type=jnp.float32)
    out_proj = jnp.dot(out_grads, out_basis, preferred_element_type=jnp.float32)
    in_low = lax.optimization_barrier(in_proj.astype(jnp.bfloat16)).astype(jnp.float32)
    out_low = lax.optimization_barrier(out_proj.astype(jnp.bfloat16)).astype(jnp.float32)
    blocks = example_ids.shape[0]
    in_rows = in_low.reshape(blocks, TOK_DEV, R)
    out_rows = out_low.reshape(blocks, TOK_DEV, R)
    labels = jnp.arange(EX_DEV, dtype=jnp.int32)
    onehot = (example_ids[:, None, :] == labels[None, :, None]).astype(jnp.float32)
    grads = jnp.einsum("bet,bti,bto->beio", onehot, in_rows, out_rows)
    grads = grads / loss_counts.astype(jnp.float32)[:, :, None, None]
    flat = grads.reshape(blocks * EX_DEV, R * R).astype(jnp.bfloat16)
    return lax.dot_general(flat, queries, (((1,), (1,)), ((), ())), preferred_element_type=jnp.float32)
```

```python
import jax
import jax.numpy as jnp
from jax import lax
from jax.sharding import PartitionSpec as P


def local(inputs, out_grads, in_basis, out_basis, example_ids, loss_counts, queries):
    tok_rows = example_ids.shape[1]
    example_count = loss_counts.shape[1]
    rank_size = in_basis.shape[1]
    parts = inputs.shape[0] // tok_rows
    left = jnp.dot(inputs, in_basis, preferred_element_type=jnp.float32)
    right = jnp.dot(out_grads, out_basis, preferred_element_type=jnp.float32)
    mine = lax.psum_scatter(jnp.concatenate([left, right], axis=1), "dp", scatter_dimension=0, tiled=True)
    low = lax.optimization_barrier(mine.astype(jnp.bfloat16)).astype(jnp.float32)
    labels = jnp.arange(example_count, dtype=jnp.int32)
    onehot = (example_ids[0][None, :] == labels[:, None]).astype(jnp.float32)
    grads = jnp.einsum("et,ti,to->eio", onehot, low[:, :rank_size], low[:, rank_size:])
    grads = grads / loss_counts[0].astype(jnp.float32)[:, None, None]
    flat = grads.reshape(example_count, rank_size * rank_size).astype(jnp.bfloat16)
    every = lax.all_gather(flat, "dp", axis=0, tiled=True)
    part = lax.dot_general(every, queries, (((1,), (1,)), ((), ())), preferred_element_type=jnp.float32)
    return lax.all_to_all(part, "dp", split_axis=0, concat_axis=1, tiled=True)


def solution(mesh):
    in_specs = (
        P("grp", "dp"),
        P("grp", "dp"),
        P("dp", None),
        P("dp", None),
        P(("grp", "dp"), None),
        P(("grp", "dp"), None),
        P("dp", None),
    )
    out_specs = P(("grp", "dp"), None)
    return jax.shard_map(local, mesh=mesh, in_specs=in_specs, out_specs=out_specs, check_vma=False)
```

```python
import functools

import jax
import jax.numpy as jnp
from jax import lax
from jax.experimental import pallas as pl
from jax.experimental.pallas import tpu as pltpu
from jax.sharding import PartitionSpec as P

MESH = pl.DeviceIdType.MESH
F32, BF16 = jnp.float32, jnp.bfloat16
NT = (((1,), (1,)), ((), ()))


def kernel(
    far, x_hbm, g_hbm, wi_ref, wo_ref, ids_ref, cnt_ref, q_hbm, out_ref,
    x_v, g_v, w_v, q_v, core_out, core_in, own, y_out, y_in, z_out, z_in, low, lhs, grads, s_out, s_in,
    x_sem, g_sem, q_sem, qs_sem, qr_sem, cs_sem, cr_sem, ys_sem, yr_sem, zs_sem, zr_sem,
    az_s, az_r, ay_s, ay_r, ss_sem, sr_sem,
):
    me = lax.axis_index("dp")
    z, y, c = me // 4, (me // 2) % 2, me % 2
    chip = me // 2
    rows = ids_ref.shape[1]
    examples = cnt_ref.shape[1]
    rank = wi_ref.shape[1]
    feats = wi_ref.shape[0]
    group = 4 * rows
    nq = q_hbm.shape[0]

    def device(zz, yy, cc):
        return {"dp": zz * 4 + yy * 2 + cc}

    def send(src, dst, ssem, rsem, target):
        copy = pltpu.make_async_remote_copy(
            src_ref=src, dst_ref=dst, send_sem=ssem, recv_sem=rsem, device_id=target, device_id_type=MESH)
        copy.start()
        return copy

    zs = [lax.rem(z + 1 + s, far) for s in range(far)]
    loads = []
    for s in range(far):
        at = pl.ds(pl.multiple_of(zs[s] * group, group), group)
        a = pltpu.make_async_copy(x_hbm.at[at, :], x_v.at[s], x_sem.at[s])
        b = pltpu.make_async_copy(g_hbm.at[at, :], g_v.at[s], g_sem.at[s])
        a.start()
        b.start()
        loads.append((a, b))

    barrier = pltpu.get_barrier_semaphore()
    pl.semaphore_signal(barrier, inc=1, device_id=device(z, y, 1 - c), device_id_type=MESH)
    for dz in range(far):
        for dy in range(2):
            if dz or dy:
                yy = 1 - y if dy else y
                pl.semaphore_signal(
                    barrier, inc=1, device_id=device(lax.rem(z + dz, far), yy, c), device_id_type=MESH)

    w_v[:feats, :] = jnp.concatenate([wi_ref[...], jnp.zeros_like(wi_ref)], axis=1)
    w_v[feats:, :] = jnp.concatenate([jnp.zeros_like(wo_ref), wo_ref[...]], axis=1)
    labels = lax.broadcasted_iota(jnp.int32, (examples, rows), 0)
    onehot = jnp.where(labels == ids_ref[...], 1.0, 0.0).astype(F32)
    low[0, 0, 2 * rank:, :] = onehot.astype(BF16)

    pl.semaphore_wait(barrier, 2 * far)

    q_rows = pl.ds(pl.multiple_of(c * nq, nq), nq)
    q_far = None
    q_near = None

    def project(s, yy, cc):
        at = pl.ds(pl.multiple_of((yy * 2 + cc) * rows, rows), rows)
        return (jnp.dot(x_v[s, at, :], w_v[:feats, :], preferred_element_type=F32)
                + jnp.dot(g_v[s, at, :], w_v[feats:, :], preferred_element_type=F32))

    core_copies, y_copies, z_copies = [], [], []

    def z_stage(s):
        core_copies[2 * s + 1].wait_recv()
        y_copies[s].wait_recv()
        total = own[2 * s + 1] + core_in[2 * s + 1] + y_in[s].astype(F32)
        if s == far - 1:
            return total
        z_out[s] = total.astype(BF16)
        z_copies.append(send(z_out.at[s], z_in.at[s], zs_sem.at[s], zr_sem.at[s], device(zs[s], y, c)))

    for s in range(far):
        loads[s][0].wait()
        loads[s][1].wait()
        for k, yy in enumerate((1 - y, y)):
            core_out[2 * s + k] = project(s, yy, 1 - c)
            core_copies.append(send(core_out.at[2 * s + k], core_in.at[2 * s + k], cs_sem.at[2 * s + k],
                                    cr_sem.at[2 * s + k], device(z, y, 1 - c)))
        for k, yy in enumerate((1 - y, y)):
            own[2 * s + k] = project(s, yy, c)
        core_copies[2 * s].wait_recv()
        y_out[s] = (own[2 * s] + core_in[2 * s]).astype(BF16)
        y_copies.append(send(y_out.at[s], y_in.at[s], ys_sem.at[s], yr_sem.at[s], device(z, 1 - y, c)))
        if s:
            z_stage(s - 1)
    q_far = send(q_hbm, q_v.at[q_rows, :], qs_sem, qr_sem, device(z, y, 1 - c))
    q_near = pltpu.make_async_copy(q_hbm, q_v.at[q_rows, :], q_sem)
    q_near.start()
    total = z_stage(far - 1)
    for s in range(far - 1):
        z_copies[s].wait_recv()
        total = total + z_in[s].astype(F32)
    low[0, 0, :2 * rank, :] = total.T.astype(BF16)

    gz = [None] * far
    gy = [None] * far
    for dz in range(1, far):
        gz[dz] = send(low.at[0, 0], low.at[dz, 0], az_s.at[dz], az_r.at[dz], device(lax.rem(z + dz, far), y, c))
    gy[0] = send(low.at[0, 0], low.at[0, 1], ay_s.at[0], ay_r.at[0], device(z, 1 - y, c))

    def outer(dz, dy):
        left = low[dz, dy, :rank, :].astype(F32)
        right = low[dz, dy, rank:2 * rank, :]
        hot = low[dz, dy, 2 * rank:, :].astype(F32)
        for i in range(rank):
            lhs[(i // 2) * examples:(i // 2 + 1) * examples, (i % 2) * rows:(i % 2 + 1) * rows] = (
                hot * left[i:i + 1, :]).astype(BF16)
        none = jnp.zeros_like(right)
        rhs = jnp.concatenate(
            [jnp.concatenate([right, none], axis=1), jnp.concatenate([none, right], axis=1)], axis=0)
        flat = lax.dot_general(lhs[...], rhs, NT, preferred_element_type=F32).astype(BF16)
        r = 2 * dz + dy
        for i in range(rank // 2):
            grads[r * examples:(r + 1) * examples, i * 2 * rank:(i + 1) * 2 * rank] = (
                flat[i * examples:(i + 1) * examples, :])

    outer(0, 0)
    for dz in range(1, far):
        gz[dz].wait_recv()
        gy[dz] = send(low.at[dz, 0], low.at[dz, 1], ay_s.at[dz], ay_r.at[dz], device(z, 1 - y, c))
        outer(dz, 0)
    for dz in range(far):
        gy[dz].wait_recv()
        outer(dz, 1)

    q_near.wait()
    q_far.wait_recv()
    scores = lax.dot_general(grads[...], q_v[...], NT, preferred_element_type=F32)
    back = []
    for dz in range(far):
        for dy in range(2):
            r = 2 * dz + dy
            block = scores[r * examples:(r + 1) * examples, :]
            if r == 0:
                s_in[chip] = block
            else:
                s_out[r] = block
                yy = 1 - y if dy else y
                back.append(send(s_out.at[r], s_in.at[chip], ss_sem.at[r], sr_sem.at[r],
                                 device(lax.rem(z - dz + far, far), yy, c)))
    diag = lax.broadcasted_iota(jnp.int32, (examples, examples), 0) == lax.broadcasted_iota(
        jnp.int32, (examples, examples), 1)
    counts = jnp.sum(jnp.where(diag, jnp.broadcast_to(cnt_ref[...].astype(F32), (examples, examples)), 0.0),
                     axis=1, keepdims=True)
    for copy in back:
        copy.wait_recv()
    for k in range(2 * far):
        out_ref[:, k * 2 * nq:(k + 1) * 2 * nq] = s_in[k] / counts
    for copy in core_copies + y_copies + z_copies + gz[1:] + gy + back + [q_far]:
        copy.wait_send()


def local(inputs, out_grads, in_basis, out_basis, example_ids, loss_counts, queries):
    rows = example_ids.shape[1]
    examples = loss_counts.shape[1]
    rank = in_basis.shape[1]
    n = inputs.shape[0] // rows
    far = n // 4
    nq, flat = queries.shape
    wide = 2 * rank
    vmem, hbm = pl.BlockSpec(memory_space=pltpu.VMEM), pl.BlockSpec(memory_space=pl.ANY)
    dma = pltpu.SemaphoreType.DMA
    feats = in_basis.shape[0] + out_basis.shape[0]
    return pl.pallas_call(
        functools.partial(kernel, far),
        out_shape=jax.ShapeDtypeStruct((examples, n * nq), F32),
        in_specs=[hbm, hbm, vmem, vmem, vmem, vmem, hbm],
        out_specs=vmem,
        scratch_shapes=[
            pltpu.VMEM((far, 4 * rows, inputs.shape[1]), BF16),
            pltpu.VMEM((far, 4 * rows, out_grads.shape[1]), BF16),
            pltpu.VMEM((feats, wide), BF16),
            pltpu.VMEM((2 * nq, flat), BF16),
            pltpu.VMEM((2 * far, rows, wide), F32),
            pltpu.VMEM((2 * far, rows, wide), F32),
            pltpu.VMEM((2 * far, rows, wide), F32),
            pltpu.VMEM((far, rows, wide), BF16),
            pltpu.VMEM((far, rows, wide), BF16),
            pltpu.VMEM((far, rows, wide), BF16),
            pltpu.VMEM((far, rows, wide), BF16),
            pltpu.VMEM((far, 2, wide + examples, rows), BF16),
            pltpu.VMEM((rank // 2 * examples, 2 * rows), BF16),
            pltpu.VMEM((2 * far * examples, flat), BF16),
            pltpu.VMEM((2 * far, examples, 2 * nq), F32),
            pltpu.VMEM((2 * far, examples, 2 * nq), F32),
            dma((far,)), dma((far,)), dma, dma, dma,
            dma((2 * far,)), dma((2 * far,)), dma((far,)), dma((far,)), dma((far,)), dma((far,)),
            dma((far,)), dma((far,)), dma((far,)), dma((far,)), dma((2 * far,)), dma((2 * far,)),
        ],
        compiler_params=pltpu.CompilerParams(
            collective_id=0, has_side_effects=True, vmem_limit_bytes=56 * 2 ** 20),
        cost_estimate=pl.CostEstimate(
            flops=2 * n * rows * feats * wide, bytes_accessed=2 * n * rows * feats, transcendentals=0),
    )(inputs, out_grads, in_basis, out_basis, example_ids, loss_counts, queries)


def solution(mesh):
    in_specs = (
        P("grp", "dp"),
        P("grp", "dp"),
        P("dp", None),
        P("dp", None),
        P(("grp", "dp"), None),
        P(("grp", "dp"), None),
        P("dp", None),
    )
    out_specs = P(("grp", "dp"), None)
    return jax.shard_map(local, mesh=mesh, in_specs=in_specs, out_specs=out_specs, check_vma=False)
```

```python
import functools

import jax
import jax.numpy as jnp
from jax import lax
from jax.experimental import pallas as pl
from jax.experimental.pallas import tpu as pltpu
from jax.sharding import PartitionSpec as P

MESH = pl.DeviceIdType.MESH
F32, BF16 = jnp.float32, jnp.bfloat16
NT = (((1,), (1,)), ((), ()))


def kernel(
    far, x_hbm, g_hbm, wi_hbm, wo_hbm, ids_ref, cnt_ref, q_hbm, out_ref,
    x_v, g_v, w_v, q_v, core_out, core_in, own, y_out, y_in, z_out, z_in, low, lhs, grads, s_out, s_in,
    x_sem, g_sem, w_sem, q_sem, qs_sem, qr_sem, cs_sem, cr_sem, ys_sem, yr_sem, zs_sem, zr_sem,
    az_s, az_r, ay_s, ay_r, ss_sem, sr_sem,
):
    me = lax.axis_index("dp")
    z, y, c = me // 4, (me // 2) % 2, me % 2
    chip = me // 2
    rows = ids_ref.shape[1]
    examples = cnt_ref.shape[1]
    rank, feats = wi_hbm.shape
    group = 4 * rows
    nq = q_hbm.shape[0]

    def device(zz, yy, cc):
        return {"dp": zz * 4 + yy * 2 + cc}

    def send(src, dst, ssem, rsem, target):
        copy = pltpu.make_async_remote_copy(
            src_ref=src, dst_ref=dst, send_sem=ssem, recv_sem=rsem, device_id=target, device_id_type=MESH)
        copy.start()
        return copy

    w_v[...] = jnp.zeros_like(w_v)
    w_copies = [
        pltpu.make_async_copy(wi_hbm, w_v.at[:rank, :feats], w_sem.at[0]),
        pltpu.make_async_copy(wo_hbm, w_v.at[rank:, feats:], w_sem.at[1]),
    ]
    for copy in w_copies:
        copy.start()
    zs = [lax.rem(z + 1 + s, far) for s in range(far)]
    loads = []
    for s in range(far):
        at = pl.ds(pl.multiple_of(zs[s] * group, group), group)
        a = pltpu.make_async_copy(x_hbm.at[at, :], x_v.at[s], x_sem.at[s])
        b = pltpu.make_async_copy(g_hbm.at[at, :], g_v.at[s], g_sem.at[s])
        a.start()
        b.start()
        loads.append((a, b))

    barrier = pltpu.get_barrier_semaphore()
    pl.semaphore_signal(barrier, inc=1, device_id=device(z, y, 1 - c), device_id_type=MESH)
    for dz in range(far):
        for dy in range(2):
            if dz or dy:
                yy = 1 - y if dy else y
                pl.semaphore_signal(
                    barrier, inc=1, device_id=device(lax.rem(z + dz, far), yy, c), device_id_type=MESH)

    labels = lax.broadcasted_iota(jnp.int32, (examples, rows), 0)
    onehot = jnp.where(labels == ids_ref[...], 1.0, 0.0).astype(F32)
    low[0, 0, 2 * rank:, :] = onehot.astype(BF16)

    pl.semaphore_wait(barrier, 2 * far)

    q_rows = pl.ds(pl.multiple_of(c * nq, nq), nq)
    q_far = None
    q_near = None

    def project(s, yy, cc):
        at = pl.ds(pl.multiple_of((yy * 2 + cc) * rows, rows), rows)
        return (lax.dot_general(x_v[s, at, :], w_v[:, :feats], NT, preferred_element_type=F32)
                + lax.dot_general(g_v[s, at, :], w_v[:, feats:], NT, preferred_element_type=F32))

    core_copies, y_copies, z_copies = [], [], []

    def z_stage(s):
        core_copies[2 * s + 1].wait_recv()
        y_copies[s].wait_recv()
        total = own[2 * s + 1] + core_in[2 * s + 1] + y_in[s].astype(F32)
        if s == far - 1:
            return total
        z_out[s] = total.astype(BF16)
        z_copies.append(send(z_out.at[s], z_in.at[s], zs_sem.at[s], zr_sem.at[s], device(zs[s], y, c)))

    for copy in w_copies:
        copy.wait()
    for s in range(far):
        loads[s][0].wait()
        loads[s][1].wait()
        for k, yy in enumerate((1 - y, y)):
            core_out[2 * s + k] = project(s, yy, 1 - c)
            core_copies.append(send(core_out.at[2 * s + k], core_in.at[2 * s + k], cs_sem.at[2 * s + k],
                                    cr_sem.at[2 * s + k], device(z, y, 1 - c)))
        for k, yy in enumerate((1 - y, y)):
            own[2 * s + k] = project(s, yy, c)
        core_copies[2 * s].wait_recv()
        y_out[s] = (own[2 * s] + core_in[2 * s]).astype(BF16)
        y_copies.append(send(y_out.at[s], y_in.at[s], ys_sem.at[s], yr_sem.at[s], device(z, 1 - y, c)))
        if s:
            z_stage(s - 1)
    q_far = send(q_hbm, q_v.at[q_rows, :], qs_sem, qr_sem, device(z, y, 1 - c))
    q_near = pltpu.make_async_copy(q_hbm, q_v.at[q_rows, :], q_sem)
    q_near.start()
    total = z_stage(far - 1)
    for s in range(far - 1):
        z_copies[s].wait_recv()
        total = total + z_in[s].astype(F32)
    low[0, 0, :2 * rank, :] = total.T.astype(BF16)

    gz = [None] * far
    gy = [None] * far
    for dz in range(1, far):
        gz[dz] = send(low.at[0, 0], low.at[dz, 0], az_s.at[dz], az_r.at[dz], device(lax.rem(z + dz, far), y, c))
    gy[0] = send(low.at[0, 0], low.at[0, 1], ay_s.at[0], ay_r.at[0], device(z, 1 - y, c))

    def outer(dz, dy):
        left = low[dz, dy, :rank, :].astype(F32)
        right = low[dz, dy, rank:2 * rank, :]
        hot = low[dz, dy, 2 * rank:, :].astype(F32)
        for i in range(rank):
            lhs[(i // 2) * examples:(i // 2 + 1) * examples, (i % 2) * rows:(i % 2 + 1) * rows] = (
                hot * left[i:i + 1, :]).astype(BF16)
        none = jnp.zeros_like(right)
        rhs = jnp.concatenate(
            [jnp.concatenate([right, none], axis=1), jnp.concatenate([none, right], axis=1)], axis=0)
        flat = lax.dot_general(lhs[...], rhs, NT, preferred_element_type=F32).astype(BF16)
        r = dy * far + dz
        for i in range(rank // 2):
            grads[r * examples:(r + 1) * examples, i * 2 * rank:(i + 1) * 2 * rank] = (
                flat[i * examples:(i + 1) * examples, :])

    back = []

    def score(dy):
        half = slice(dy * far * examples, (dy + 1) * far * examples)
        scores = lax.dot_general(grads[half, :], q_v[...], NT, preferred_element_type=F32)
        yy = 1 - y if dy else y
        for dz in range(far):
            r = dy * far + dz
            part = scores[dz * examples:(dz + 1) * examples, :]
            if r == 0:
                s_in[chip] = part
            else:
                s_out[r] = part
                back.append(send(s_out.at[r], s_in.at[chip], ss_sem.at[r], sr_sem.at[r],
                                 device(lax.rem(z - dz + far, far), yy, c)))

    outer(0, 0)
    for dz in range(1, far):
        gz[dz].wait_recv()
        gy[dz] = send(low.at[dz, 0], low.at[dz, 1], ay_s.at[dz], ay_r.at[dz], device(z, 1 - y, c))
        outer(dz, 0)
    q_near.wait()
    q_far.wait_recv()
    score(0)
    for dz in range(far):
        gy[dz].wait_recv()
        outer(dz, 1)
    score(1)
    diag = lax.broadcasted_iota(jnp.int32, (examples, examples), 0) == lax.broadcasted_iota(
        jnp.int32, (examples, examples), 1)
    counts = jnp.sum(jnp.where(diag, jnp.broadcast_to(cnt_ref[...].astype(F32), (examples, examples)), 0.0),
                     axis=1, keepdims=True)
    for copy in back:
        copy.wait_recv()
    for k in range(2 * far):
        out_ref[:, k * 2 * nq:(k + 1) * 2 * nq] = s_in[k] / counts
    for copy in core_copies + y_copies + z_copies + gz[1:] + gy + back + [q_far]:
        copy.wait_send()


def local(inputs, out_grads, in_basis, out_basis, example_ids, loss_counts, queries):
    rows = example_ids.shape[1]
    examples = loss_counts.shape[1]
    rank = in_basis.shape[1]
    n = inputs.shape[0] // rows
    far = n // 4
    nq, flat = queries.shape
    wide = 2 * rank
    vmem, hbm = pl.BlockSpec(memory_space=pltpu.VMEM), pl.BlockSpec(memory_space=pl.ANY)
    dma = pltpu.SemaphoreType.DMA
    feats = in_basis.shape[0] + out_basis.shape[0]
    return pl.pallas_call(
        functools.partial(kernel, far),
        out_shape=jax.ShapeDtypeStruct((examples, n * nq), F32),
        in_specs=[hbm, hbm, hbm, hbm, vmem, vmem, hbm],
        out_specs=vmem,
        scratch_shapes=[
            pltpu.VMEM((far, 4 * rows, inputs.shape[1]), BF16),
            pltpu.VMEM((far, 4 * rows, out_grads.shape[1]), BF16),
            pltpu.VMEM((wide, feats), BF16),
            pltpu.VMEM((2 * nq, flat), BF16),
            pltpu.VMEM((2 * far, rows, wide), F32),
            pltpu.VMEM((2 * far, rows, wide), F32),
            pltpu.VMEM((2 * far, rows, wide), F32),
            pltpu.VMEM((far, rows, wide), BF16),
            pltpu.VMEM((far, rows, wide), BF16),
            pltpu.VMEM((far, rows, wide), BF16),
            pltpu.VMEM((far, rows, wide), BF16),
            pltpu.VMEM((far, 2, wide + examples, rows), BF16),
            pltpu.VMEM((rank // 2 * examples, 2 * rows), BF16),
            pltpu.VMEM((2 * far * examples, flat), BF16),
            pltpu.VMEM((2 * far, examples, 2 * nq), F32),
            pltpu.VMEM((2 * far, examples, 2 * nq), F32),
            dma((far,)), dma((far,)), dma((2,)), dma, dma, dma,
            dma((2 * far,)), dma((2 * far,)), dma((far,)), dma((far,)), dma((far,)), dma((far,)),
            dma((far,)), dma((far,)), dma((far,)), dma((far,)), dma((2 * far,)), dma((2 * far,)),
        ],
        compiler_params=pltpu.CompilerParams(
            collective_id=0, has_side_effects=True, vmem_limit_bytes=56 * 2 ** 20),
        cost_estimate=pl.CostEstimate(
            flops=2 * n * rows * feats * wide, bytes_accessed=2 * n * rows * feats, transcendentals=0),
    )(inputs, out_grads, in_basis.T, out_basis.T, example_ids, loss_counts, queries)


def solution(mesh):
    in_specs = (
        P("grp", "dp"),
        P("grp", "dp"),
        P("dp", None),
        P("dp", None),
        P(("grp", "dp"), None),
        P(("grp", "dp"), None),
        P("dp", None),
    )
    out_specs = P(("grp", "dp"), None)
    return jax.shard_map(local, mesh=mesh, in_specs=in_specs, out_specs=out_specs, check_vma=False)
```
